32 devices in a mesh: row: 4 (over y, core), col: 8 (over z, x).
Axes of the slice: x: 2, y: 2, z: 4, core: 2. Of those that a mesh axis runs over, the one named last changes fastest.
Arguments:
- user_emb: float32 [4, 8, 2048, 128], P('row', 'col'), may hold values from -2.4 to 2.4
- item_emb: float32 [8, 4, 1024, 128], P('col', 'row'), may hold values from -2.4 to 2.4
- tile_vals: bfloat16 [4, 8, 512, 128, 128], P('row', 'col'), may hold values from 0 to 0.029907227
- tile_rows: int32 [4, 8, 512], P('row', 'col'), may hold values from 0 to 127
- tile_cols: int32 [4, 8, 512], P('row', 'col'), may hold values from 0 to 31
- tile_count: int32 [4, 8], P('row', 'col'), may hold values from 128 to 512, as said below
- pair_users: int32 [16384], P(('row', 'col')), may hold values from 0 to 65535, as said below
- pair_items: int32 [16384], P(('row', 'col')), may hold values from 0 to 32767, as said below
- negatives: int32 [1024], replicated, may hold values from 0 to 32767, as said below
Outputs:
- user_final: float32 [4, 8, 2048, 128], P('row', 'col')
- item_final: float32 [8, 4, 1024, 128], P('col', 'row')
- bpr_terms: float32 [16384, 1024], P(('row', 'col'))
The draws below stay inside these ranges and needn't reach their ends.
Inputs may be any that keep to these rules, and one draw needn't show every extreme that they name: `pair_users`: taken in aligned blocks of 512 entries, at most 32 entries of one block name users that one device holds in user_emb; in every draw some device's users are named exactly 32 times in every block. `pair_items`: taken in aligned blocks of 512 entries, at most 32 entries of one block name items that one device holds in item_emb; in every draw some device's items are named exactly 32 times in every block. `tile_count`: some block has all 512 slots live. `negatives`: entry j names an item that the device with row index (j // 32) // 8 and col index (j // 32) % 8 holds in item_emb.
All inputs are finite; a program needn't handle non-finite values.
Results may differ from the reference program's by a relative error of at most 0.009.
Values may be sent and summed in bfloat16 or wider, within the bound.
No kernel may reach another device: no remote copies, remote signals or barrier semaphores. Data moves between devices by JAX's collectives and lax.ppermute only.
A program may use at most 128 MiB of HBM per device.

```python
import jax
import jax.numpy as jnp
from jax import lax

E = 128
TILE = 128
UDEV = 2048
IDEV = 1024
TILES_DEV = 512
PAIRS_DEV = 512
NEG = 1024
PAIRS = 16384
TROWS = 128
TCOLS = 32
N_ROW = 4
N_COL = 8


def owner_blocks(key):
    devices = N_ROW * N_COL
    common = jax.random.randint(jax.random.fold_in(key, 1), (), 0, devices)

    def one_block(subkey):
        first, second = jax.random.split(subkey)
        emptied = (common + jax.random.randint(first, (), 1, devices)) % devices
        owners = jnp.arange(PAIRS_DEV, dtype=jnp.int32) % devices
        owners = jnp.where(owners == emptied, common, owners)
        return jax.random.permutation(second, owners)
    subkeys = jax.random.split(jax.random.fold_in(key, 2), devices)
    return jax.vmap(one_block)(subkeys).reshape(-1)


def draw_pair_users(key, part):
    owners = owner_blocks(jax.random.fold_in(key, 11))
    local = jax.random.randint(jax.random.fold_in(key, 12), (PAIRS,), 0, UDEV)
    return (owners * UDEV + local).astype(jnp.int32)


def draw_pair_items(key, part):
    owners = owner_blocks(jax.random.fold_in(key, 21))
    local = jax.random.randint(jax.random.fold_in(key, 22), (PAIRS,), 0, IDEV)
    holder = owners % N_COL * N_ROW + owners // N_COL
    return (holder * IDEV + local).astype(jnp.int32)


def draw_tile_count(key, part):
    counts = jax.random.randint(jax.random.fold_in(key, 31), (N_ROW * N_COL,), TILES_DEV // 4, TILES_DEV + 1)
    chosen = jax.random.randint(jax.random.fold_in(key, 32), (), 0, N_ROW * N_COL)
    counts = counts.at[chosen].set(TILES_DEV)
    return counts.reshape(N_ROW, N_COL).astype(jnp.int32)


def draw_negatives(key, part):
    per_device = NEG // (N_ROW * N_COL)
    device = jnp.arange(NEG, dtype=jnp.int32) // per_device
    holder = device % N_COL * N_ROW + device // N_COL
    local = jax.random.randint(jax.random.fold_in(key, 41), (NEG,), 0, IDEV)
    return (holder * IDEV + local).astype(jnp.int32)


def set_ends(array, own_key, least, high):
    longest = array.shape.index(max(array.shape))
    spots = []
    for shift in (0, 1):
        where = [jax.random.randint(jax.random.fold_in(own_key, axis), (), 0, length) for axis, length in enumerate(array.shape)]
        where[longest] = (where[longest] + shift) % array.shape[longest]
        spots.append(tuple(where))
    return array.at[spots[0]].set(least).at[spots[1]].set(high)


def steps_of(stream_key, extent, cuts, least, top_value):
    level, own = 1.0, jax.random.fold_in(stream_key, 6)
    for position, blocks in cuts:
        steps = jnp.exp(jax.random.uniform(jax.random.fold_in(own, position), (blocks,), jnp.float32, least / len(cuts), top_value / len(cuts)))
        level = level * jnp.repeat(steps, extent[position] // blocks).reshape([-1 if axis == position else 1 for axis in range(len(extent))])
    return level


def bell_draw(rng, dims, scale, limit, shards=(), kind=jnp.bfloat16):
    result = scale * jax.random.normal(rng, dims, jnp.float32)
    if shards:
        result = result * steps_of(rng, dims, shards, -0.22, 0.18)
    return jnp.clip(result, -limit, limit).astype(kind)


def setup_inputs(seed: int = 0) -> dict:
    seeds = jax.random.split(jax.random.key(seed), 10)
    user_emb = bell_draw(seeds[0], (N_ROW, N_COL, UDEV, E), 0.4, 2.4, ((0, 4), (1, 8)), jnp.float32)
    item_emb = bell_draw(seeds[1], (N_COL, N_ROW, IDEV, E), 0.4, 2.4, ((0, 8), (1, 4)), jnp.float32)
    tile_vals = jnp.clip(0.029907227 * jax.random.uniform(seeds[2], (N_ROW, N_COL, TILES_DEV, TILE, TILE), jnp.float32) ** steps_of(seeds[2], (N_ROW, N_COL, TILES_DEV, TILE, TILE), ((0, 4), (1, 8)), -0.2, 0.2), 0.0, 0.029907227).astype(jnp.bfloat16)
    tile_rows = set_ends(jax.random.randint(seeds[3], (N_ROW, N_COL, TILES_DEV), 0, TROWS), jax.random.fold_in(seeds[3], 1), 0, TROWS - 1).astype(jnp.int32)
    tile_cols = set_ends(jax.random.randint(seeds[4], (N_ROW, N_COL, TILES_DEV), 0, TCOLS), jax.random.fold_in(seeds[4], 1), 0, TCOLS - 1).astype(jnp.int32)
    tile_count = draw_tile_count(jax.random.fold_in(seeds[9], 71), 0)
    pair_users = draw_pair_users(jax.random.fold_in(seeds[9], 71), 0)
    pair_items = draw_pair_items(jax.random.fold_in(seeds[9], 71), 0)
    negatives = draw_negatives(jax.random.fold_in(seeds[9], 71), 0)
    return dict(user_emb=user_emb, item_emb=item_emb, tile_vals=tile_vals, tile_rows=tile_rows, tile_cols=tile_cols, tile_count=tile_count, pair_users=pair_users, pair_items=pair_items, negatives=negatives)


def rounded(values):
    return lax.optimization_barrier(values.astype(jnp.bfloat16)).astype(jnp.float32)


def reference(user_emb, item_emb, tile_vals, tile_rows, tile_cols, tile_count, pair_users, pair_items, negatives):
    user_low = rounded(user_emb)
    item_low = rounded(item_emb)
    row_tiles = N_COL * UDEV // TILE
    col_tiles = N_ROW * IDEV // TILE

    def visit(totals, device):
        user_prop, item_prop = totals
        row_block = device // N_COL
        col_block = device % N_COL
        values = tile_vals[row_block, col_block].astype(jnp.float32)
        row_ids = tile_rows[row_block, col_block]
        col_ids = tile_cols[row_block, col_block]
        live = (jnp.arange(TILES_DEV, dtype=jnp.int32) < tile_count[row_block, col_block]).astype(jnp.float32)[:, None, None]
        user_tiles = user_low[row_block].reshape(row_tiles, TILE, E)
        item_tiles = item_low[col_block].reshape(col_tiles, TILE, E)
        to_users = jnp.einsum("tij,tje->tie", values, item_tiles[col_ids]) * live
        to_items = jnp.einsum("tij,tie->tje", values, user_tiles[row_ids]) * live
        user_add = rounded(jnp.zeros((row_tiles, TILE, E), jnp.float32).at[row_ids].add(to_users))
        item_add = rounded(jnp.zeros((col_tiles, TILE, E), jnp.float32).at[col_ids].add(to_items))
        user_prop = user_prop.at[row_block].add(user_add.reshape(N_COL, UDEV, E))
        item_prop = item_prop.at[col_block].add(item_add.reshape(N_ROW, IDEV, E))
        return (user_prop, item_prop), None

    start = (jnp.zeros(user_emb.shape, jnp.float32), jnp.zeros(item_emb.shape, jnp.float32))
    (user_prop, item_prop), _ = lax.scan(visit, start, jnp.arange(N_ROW * N_COL, dtype=jnp.int32))
    user_final = (user_emb + user_prop) * 0.5
    item_final = (item_emb + item_prop) * 0.5
    user_flat = user_final.reshape(-1, E)
    item_flat = item_final.reshape(-1, E)
    user_vec = user_flat[pair_users]
    item_vec = item_flat[pair_items]
    negative_vec = item_flat[negatives]
    positive = jnp.sum(user_vec * item_vec, axis=1)
    against = jnp.dot(user_vec, negative_vec.T, precision=lax.Precision.HIGHEST)
    bpr_terms = jnp.log1p(jnp.exp(against - positive[:, None]))
    return user_final, item_final, bpr_terms
```

```python
import functools

import jax
import jax.numpy as jnp
from jax import lax
from jax.experimental import pallas as pl
from jax.experimental.pallas import tpu as pltpu
from jax.sharding import PartitionSpec as P

F32 = jnp.float32
BF16 = jnp.bfloat16
VMEM_WHOLE = pl.BlockSpec(memory_space=pltpu.VMEM)


def split_axis(size):
    fast = max(d for d in range(1, size + 1) if size % d == 0 and d * d <= size)
    return size // fast, fast


def arrivals(slow):
    return [sorted(range(slow), key=lambda t: (abs(t - z), t < z)) for z in range(slow)]


def moves(slow, fast, step):
    pairs = []
    for z in range(slow):
        for x in range(fast):
            to = step(z, x)
            if to is not None:
                pairs.append((z * fast + x, to[0] * fast + to[1]))
    return pairs


def choose(place, options):
    picked = None
    seen = []
    for z, option in enumerate(options):
        if option is None or any(option is other for other, _ in seen):
            continue
        seen.append((option, [i for i, o in enumerate(options) if o is option]))
    for option, places in seen:
        if picked is None:
            picked = option
            continue
        here = functools.reduce(jnp.logical_or, [place == i for i in places])
        picked = jnp.where(here, option, picked)
    return picked


def group_of(slots):
    return next(g for g in (32, 16, 8, 4, 2, 1) if slots % g == 0)


def add_tiles(count, first, group, unroll, left, right, place, trash, total):
    live = jnp.clip(count - first, 0, group)

    def some(step, carry):
        products, places = [], []
        for u in range(unroll):
            slot = step * unroll + u
            whole = first + slot
            products.append(jnp.dot(left(slot, whole), right(slot, whole), preferred_element_type=F32))
            places.append(jnp.where(slot < live, place(whole), trash))
        for product, at in zip(products, places):
            total[at] += product
        return carry

    lax.fori_loop(0, (live + unroll - 1) // unroll, some, 0)


def user_term_kernel(count_ref, rows_ref, cols_ref, base_ref, vals_ref, item_ref, *rest, group, unroll, trash):
    *outs, total = rest
    step = pl.program_id(0)

    @pl.when(step == 0)
    def _():
        total[...] = jnp.zeros_like(total)

    add_tiles(
        count_ref[0],
        step * group,
        group,
        unroll,
        lambda slot, whole: vals_ref[slot],
        lambda slot, whole: item_ref[cols_ref[whole]],
        lambda whole: rows_ref[whole],
        trash,
        total,
    )

    @pl.when(step == pl.num_programs(0) - 1)
    def _():
        for n, out in enumerate(outs):

            def tile(i, carry, n=n, out=out):
                out[i] = total[base_ref[n] + i].astype(BF16)
                return carry

            lax.fori_loop(0, out.shape[0], tile, 0, unroll=2)


def item_term_kernel(count_ref, rows_ref, cols_ref, in_base_ref, out_base_ref, vals_ref, *rest, blocks, group, unroll, trash):
    users = rest[:blocks]
    outs = rest[blocks:-3]
    table, total, sems = rest[-3:]
    step = pl.program_id(0)

    @pl.when(step == 0)
    def _():
        copies = [
            pltpu.make_async_copy(user, table.at[pl.ds(in_base_ref[n], user.shape[0])], sems.at[n])
            for n, user in enumerate(users)
        ]
        for copy in copies:
            copy.start()
        total[...] = jnp.zeros_like(total)
        for copy in copies:
            copy.wait()

    add_tiles(
        count_ref[0],
        step * group,
        group,
        unroll,
        lambda slot, whole: table[rows_ref[whole]],
        lambda slot, whole: vals_ref[slot],
        lambda whole: cols_ref[whole],
        trash,
        total,
    )

    @pl.when(step == pl.num_programs(0) - 1)
    def _():
        for n, out in enumerate(outs):

            def tile(i, carry, n=n, out=out):
                out[i] = total[out_base_ref[n] + i].astype(BF16)
                return carry

            lax.fori_loop(0, out.shape[0], tile, 0, unroll=2)


def values_spec(group, side):
    def where(i, count, *_):
        return (jnp.minimum(i, jnp.maximum(count[0] - 1, 0) // group), 0, 0)

    return pl.BlockSpec((group, side, side), where)


def user_terms(count, rows, cols, base, vals, items, tiles, outs, out_tiles):
    slots, side = vals.shape[0], vals.shape[1]
    embed = items.shape[-1]
    group = group_of(slots)
    unroll = min(8, group)
    return pl.pallas_call(
        functools.partial(user_term_kernel, group=group, unroll=unroll, trash=tiles),
        grid_spec=pltpu.PrefetchScalarGridSpec(
            num_scalar_prefetch=4,
            grid=(slots // group,),
            in_specs=[values_spec(group, side), pl.BlockSpec(items.shape, lambda i, *_: (0, 0, 0))],
            out_specs=[pl.BlockSpec((out_tiles, side, embed), lambda i, *_: (0, 0, 0)) for _ in range(outs)],
            scratch_shapes=[pltpu.VMEM((tiles + 1, side, embed), F32)],
        ),
        out_shape=[jax.ShapeDtypeStruct((out_tiles, side, embed), BF16) for _ in range(outs)],
        compiler_params=pltpu.CompilerParams(
            dimension_semantics=("arbitrary",), vmem_limit_bytes=32 * 2**20
        ),
        cost_estimate=pl.CostEstimate(
            flops=2 * slots * side * side * embed, bytes_accessed=2 * slots * side * side, transcendentals=0
        ),
        name="user_terms",
    )(count, rows, cols, base, vals, items)


def item_terms(count, rows, cols, in_base, out_base, vals, users, tiles, outs, out_tiles):
    slots, side = vals.shape[0], vals.shape[1]
    embed = users[0].shape[1]
    group = group_of(slots)
    unroll = min(8, group)
    table = len(users) * users[0].shape[0]
    return pl.pallas_call(
        functools.partial(item_term_kernel, blocks=len(users), group=group, unroll=unroll, trash=tiles),
        grid_spec=pltpu.PrefetchScalarGridSpec(
            num_scalar_prefetch=5,
            grid=(slots // group,),
            in_specs=[values_spec(group, side)] + [pl.BlockSpec(memory_space=pl.ANY) for _ in users],
            out_specs=[pl.BlockSpec((out_tiles, embed, side), lambda i, *_: (0, 0, 0)) for _ in range(outs)],
            scratch_shapes=[
                pltpu.VMEM((table, embed, side), BF16),
                pltpu.VMEM((tiles + 1, embed, side), F32),
                pltpu.SemaphoreType.DMA((len(users),)),
            ],
        ),
        out_shape=[jax.ShapeDtypeStruct((out_tiles, embed, side), BF16) for _ in range(outs)],
        compiler_params=pltpu.CompilerParams(
            dimension_semantics=("arbitrary",), vmem_limit_bytes=32 * 2**20
        ),
        cost_estimate=pl.CostEstimate(
            flops=2 * slots * side * side * embed, bytes_accessed=2 * slots * side * side, transcendentals=0
        ),
        name="item_terms",
    )(count, rows, cols, in_base, out_base, vals, *users)


def picked_rows(wanted_ref, low, out_ref, chunk):
    rows = low.shape[0]
    for at in range(0, wanted_ref.shape[0], chunk):
        some = min(chunk, wanted_ref.shape[0] - at)
        hot = wanted_ref[pl.ds(at, some), :] == lax.broadcasted_iota(jnp.int32, (some, rows), 1)
        out_ref[pl.ds(at, some), :] = jnp.dot(hot.astype(BF16), low, preferred_element_type=F32).astype(BF16)


def combine_kernel(emb_ref, wanted_ref, *rest, terms, transposed):
    parts = rest[:terms]
    final_ref, rows_ref = rest[terms:]
    side = parts[0].shape[-2]
    for i in range(parts[0].shape[0]):
        at = pl.ds(i * side, side)
        prop = functools.reduce(jnp.add, [part[i].astype(F32) for part in parts])
        if transposed:
            prop = prop.T
        final_ref[at, :] = (emb_ref[at, :] + prop) * 0.5
    picked_rows(wanted_ref, final_ref[...].astype(BF16), rows_ref, 256)


def combine(emb, parts, wanted, transposed, name):
    return pl.pallas_call(
        functools.partial(combine_kernel, terms=len(parts), transposed=transposed),
        in_specs=[VMEM_WHOLE] * (2 + len(parts)),
        out_specs=[VMEM_WHOLE] * 2,
        out_shape=[
            jax.ShapeDtypeStruct(emb.shape, F32),
            jax.ShapeDtypeStruct((wanted.shape[0], emb.shape[1]), BF16),
        ],
        compiler_params=pltpu.CompilerParams(vmem_limit_bytes=32 * 2**20),
        name=name,
    )(emb, wanted, *parts)


def bpr_kernel(user_slot_ref, item_slot_ref, users_ref, items_ref, negatives_ref, out_ref):
    def vectors(slot_ref, rows_ref):
        hot = slot_ref[...] == lax.broadcasted_iota(jnp.int32, (slot_ref.shape[0], rows_ref.shape[0]), 1)
        return jnp.dot(hot.astype(BF16), rows_ref[...], preferred_element_type=F32)

    users = vectors(user_slot_ref, users_ref)
    items = vectors(item_slot_ref, items_ref)
    positive = jnp.sum(users * items, axis=1, keepdims=True)
    against = lax.dot_general(
        users.astype(BF16), negatives_ref[...], (((1,), (1,)), ((), ())), preferred_element_type=F32
    )
    out_ref[...] = jnp.log1p(jnp.exp(against - positive))


def bpr(user_slot, item_slot, users, items, negatives):
    pairs, embed = user_slot.shape[0], users.shape[1]
    block = next(b for b in (128, 64, 32, 16, 8, pairs) if pairs % b == 0)
    whole = lambda array: pl.BlockSpec(array.shape, lambda i: (0, 0))
    return pl.pallas_call(
        bpr_kernel,
        grid=(pairs // block,),
        in_specs=[pl.BlockSpec((block, 1), lambda i: (i, 0))] * 2 + [whole(users), whole(items), whole(negatives)],
        out_specs=pl.BlockSpec((block, negatives.shape[0]), lambda i: (i, 0)),
        out_shape=jax.ShapeDtypeStruct((pairs, negatives.shape[0]), F32),
        compiler_params=pltpu.CompilerParams(
            dimension_semantics=("arbitrary",), vmem_limit_bytes=32 * 2**20
        ),
        name="bpr_terms",
    )(user_slot, item_slot, users, items, negatives)


def place_requests(owner, local, slots):
    pairs = owner.shape[0]
    order = jnp.arange(pairs, dtype=jnp.int32)
    same = (owner[:, None] == owner[None, :]) & (order[None, :] < order[:, None])
    slot = owner * slots + jnp.sum(same.astype(jnp.int32), axis=1)
    return slot


def requests_of(slot, local, total):
    hits = slot[:, None] == jnp.arange(total, dtype=jnp.int32)[None, :]
    return jnp.sum(jnp.where(hits, local[:, None], 0), axis=0)


def on_device(user_emb, item_emb, tile_vals, tile_rows, tile_cols, tile_count, pair_users, pair_items, negatives):
    row_count, col_count = lax.axis_size("row"), lax.axis_size("col")
    row, col = lax.axis_index("row"), lax.axis_index("col")
    devices = row_count * col_count
    user_dev, embed = user_emb.shape[2:]
    item_dev = item_emb.shape[2]
    side = tile_vals.shape[-1]
    user_tiles, item_tiles = user_dev // side, item_dev // side
    slow, fast = split_axis(col_count)
    z, x = col // fast, col % fast
    row_slow, row_fast = split_axis(row_count) if row_count % 2 else (row_count // 2, 2)
    y, core = row // row_fast, row % row_fast

    user_mine, item_mine = user_emb[0, 0], item_emb[0, 0]
    count, rows, cols = tile_count[0], tile_rows[0, 0], tile_cols[0, 0]
    vals = tile_vals[0, 0]
    user_low = jnp.swapaxes(user_mine.astype(BF16).reshape(user_tiles, side, embed), 1, 2)
    item_low = item_mine.astype(BF16).reshape(item_tiles, side, embed)

    def send_col(array, step):
        return lax.ppermute(array, "col", moves(slow, fast, step))

    def send_row(array, step):
        return lax.ppermute(array, "row", moves(row_slow, row_fast, step))

    halves = [item_low]
    for j in range(1, row_slow):
        halves.append(send_row(item_low, lambda a, b, j=j: ((a + j) % row_slow, b)))
    item_blocks = {(j, 0): half for j, half in enumerate(halves)}
    for i in range(1, row_fast):
        for j, half in enumerate(halves):
            item_blocks[j, i] = send_row(half, lambda a, b, i=i: (a, (b + i) % row_fast))
    item_parts = jnp.stack([item_blocks[j, i] for j in range(row_slow) for i in range(row_fast)])
    item_order = jnp.stack(
        [
            (y - row_id // row_fast) % row_slow * row_fast + (core - row_id % row_fast) % row_fast
            for row_id in range(row_count)
        ]
    )
    item_table = item_parts.reshape(row_count * item_tiles, side, embed)
    col_owner, col_within = cols // item_tiles, cols % item_tiles
    owner_y, owner_core = col_owner // row_fast, col_owner % row_fast
    near_cols = ((y - owner_y) % row_slow * row_fast + (core - owner_core) % row_fast) * item_tiles + col_within

    order = arrivals(slow)
    up, down = {0: user_low}, {0: user_low}
    user_blocks = []
    order_table = jnp.asarray(order, jnp.int32)
    for k in range(slow):
        if k:
            up[k] = send_col(up[k - 1], lambda a, b, k=k: (a + 1, b) if k - 1 <= a < slow - 1 else None)
            down[k] = send_col(down[k - 1], lambda a, b, k=k: (a - 1, b) if 0 < a <= slow - k else None)
    for k in range(slow):
        sources = []
        for place in range(slow):
            other = order[place][k]
            sources.append(up[place - other] if other <= place else down[other - place])
        block = choose(z, sources)
        user_blocks.append((block, order_table[z, k] * fast + x))
        for j in range(1, fast):
            moved = send_col(block, lambda a, b, j=j: (a, (b + j) % fast))
            user_blocks.append((moved, order_table[z, k] * fast + (x - j) % fast))
    in_base = jnp.stack([place for _, place in user_blocks]) * user_tiles

    out_places = []
    for k in range(slow):
        for j in range(fast):
            out_places.append(order_table[z, slow - 1 - k] * fast + (x + j) % fast)
    out_base = jnp.stack(out_places) * user_tiles
    user_parts = user_terms(
        count, rows, near_cols, out_base, vals, item_table, col_count * user_tiles, col_count, user_tiles
    )
    sums = []
    for k in range(slow):
        keep = user_parts[k * fast]
        others = [
            send_col(user_parts[k * fast + j], lambda a, b, j=j: (a, (b + j) % fast)) for j in range(1, fast)
        ]
        if k < slow - 1:
            total = functools.reduce(jnp.add, [part.astype(F32) for part in [keep] + others]).astype(BF16)
            sums.append(total)
        else:
            sums.append([keep] + others)
    rising = falling = None
    for step in range(1, slow):
        far = slow - step

        def onward(sign, before, far=far):
            picks = []
            for place in range(slow):
                target = place + sign * far
                picks.append(sums[slow - 1 - order[place].index(target)] if 0 <= target < slow else None)
            mine = choose(z, picks)
            if before is not None:
                mine = (mine.astype(F32) + before.astype(F32)).astype(BF16)
            return send_col(mine, lambda a, b: (a + sign, b) if 0 <= a + sign * far < slow else None)

        rising, falling = onward(1, rising), onward(-1, falling)
    user_terms_in = sums[-1] + ([rising, falling] if slow > 1 else [])

    item_places = [
        (y + j) % row_slow * row_fast + (core + i) % row_fast for j in range(row_slow) for i in range(row_fast)
    ]
    item_base = jnp.stack(item_places) * item_tiles
    item_out = item_terms(
        count,
        rows,
        cols,
        in_base,
        item_base,
        vals,
        [block for block, _ in user_blocks],
        row_count * item_tiles,
        row_count,
        item_tiles,
    )
    item_sums = []
    for j in range(row_slow):
        mine = [item_out[j * row_fast]] + [
            send_row(item_out[j * row_fast + i], lambda a, b, i=i: (a, (b + i) % row_fast))
            for i in range(1, row_fast)
        ]
        if j:
            total = functools.reduce(jnp.add, [part.astype(F32) for part in mine]).astype(BF16)
            item_sums.append(send_row(total, lambda a, b, j=j: ((a + j) % row_slow, b)))
        else:
            item_sums += mine

    slots = 2 * pair_users.shape[0] // devices
    user_owner, user_local = pair_users // user_dev, pair_users % user_dev
    item_holder, item_local = pair_items // item_dev, pair_items % item_dev
    item_owner = item_holder % row_count * col_count + item_holder // row_count
    user_slot = place_requests(user_owner, user_local, slots)
    item_slot = place_requests(item_owner, item_local, slots)
    asked = jnp.stack(
        [
            requests_of(user_slot, user_local, devices * slots).reshape(devices, slots),
            requests_of(item_slot, item_local, devices * slots).reshape(devices, slots),
        ],
        axis=1,
    )
    wanted = lax.all_to_all(asked, ("row", "col"), split_axis=0, concat_axis=0, tiled=True)
    neg_each = negatives.shape[0] // devices
    offset = (col * row_count + row) * item_dev
    named = lax.dynamic_slice_in_dim(negatives, (row * col_count + col) * neg_each, neg_each, 0) - offset

    user_wanted = wanted[:, 0].reshape(-1, 1)
    item_wanted = jnp.concatenate([wanted[:, 1].reshape(-1), named]).reshape(-1, 1)

    item_final, item_rows = combine(item_mine, item_sums, item_wanted, True, "item_final")
    asked_rows = item_rows[: devices * slots].reshape(devices, slots, embed)
    named_rows = jnp.broadcast_to(item_rows[None, devices * slots :], (devices, neg_each, embed))
    item_back = lax.all_to_all(
        jnp.concatenate([asked_rows, named_rows], axis=1), ("row", "col"), split_axis=0, concat_axis=0, tiled=True
    )
    item_table_back = item_back[:, :slots].reshape(devices * slots, embed)
    negative_rows = item_back[:, slots:].reshape(devices * neg_each, embed)

    user_final, user_rows = combine(user_mine, user_terms_in, user_wanted, False, "user_final")
    user_back = lax.all_to_all(
        user_rows.reshape(devices, slots, embed), ("row", "col"), split_axis=0, concat_axis=0, tiled=True
    ).reshape(devices * slots, embed)
    bpr_terms = bpr(user_slot[:, None], item_slot[:, None], user_back, item_table_back, negative_rows)
    return user_final.reshape(user_emb.shape), item_final.reshape(item_emb.shape), bpr_terms


def solution(mesh):
    placed = (
        P("row", "col", None, None),
        P("col", "row", None, None),
        P("row", "col", None, None, None),
        P("row", "col", None),
        P("row", "col", None),
        P("row", "col"),
        P(("row", "col")),
        P(("row", "col")),
        P(),
    )
    return jax.shard_map(
        on_device,
        mesh=mesh,
        in_specs=placed,
        out_specs=(
            P("row", "col", None, None),
            P("col", "row", None, None),
            P(("row", "col"), None),
        ),
        check_vma=False,
    )
```

```python
import functools

import jax
import jax.numpy as jnp
import numpy as np
from jax import lax
from jax.experimental import pallas as pl
from jax.experimental.pallas import tpu as pltpu
from jax.sharding import PartitionSpec as P

F32 = jnp.float32
BF16 = jnp.bfloat16
VMEM_WHOLE = pl.BlockSpec(memory_space=pltpu.VMEM)


def split_axis(size):
    fast = max(d for d in range(1, size + 1) if size % d == 0 and d * d <= size)
    return size // fast, fast


def ring_of(size):
    slow, fast = split_axis(size)
    walk = [(a, 0) for a in range(slow)]
    for turn, a in enumerate(reversed(range(slow))):
        across = range(1, fast)
        walk += [(a, b) for b in (across if turn % 2 == 0 else reversed(across))]
    return [a * fast + b for a, b in walk]


def group_of(slots):
    return next(g for g in (64, 32, 16, 8, 4, 2, 1) if slots % g == 0)


def add_tiles(count, vals_hbm, held, sems, left, right, place, trash, total, before):
    most = sems.shape[0]
    group = held.shape[0] // most
    groups = (count + group - 1) // group

    def fetch(number):
        some = pl.ds(number * group, group)
        return pltpu.make_async_copy(vals_hbm.at[some], held.at[some], sems.at[number])

    def fetch_all(numbers):
        for number in numbers:

            @pl.when(number < groups)
            def _(number=number):
                fetch(number).start()

    fetch_all(range(1))
    total[...] = jnp.zeros_like(total)
    for copy in before:
        copy.wait()
    fetch_all(range(1, most))

    def one_group(number, carry):
        fetch(number).wait()
        products, places = [], []
        for u in range(group):
            slot = number * group + u
            products.append(jnp.dot(left(slot), right(slot), preferred_element_type=F32))
            places.append(jnp.where(slot < count, place(slot), trash))
        for product, at in zip(products, places):
            total[at] += product
        return carry

    lax.fori_loop(0, groups, one_group, 0)


def hand_out(total, bases, outs):
    for n, out in enumerate(outs):

        def tile(i, carry, n=n, out=out):
            out[i] = total[bases[n] + i].astype(BF16)
            return carry

        lax.fori_loop(0, out.shape[0], tile, 0, unroll=min(8, out.shape[0]))


def fill(table, bases, blocks, sems):
    copies = [
        pltpu.make_async_copy(block, table.at[pl.ds(base, block.shape[0])], sems.at[n])
        for n, (base, block) in enumerate(zip(bases, blocks))
    ]
    for copy in copies:
        copy.start()
    return copies


def term_kernel(count_ref, rows_ref, cols_ref, in_ref, out_ref, vals_ref, *rest, axes, blocks, trash, to_users):
    given = rest[:blocks]
    *outs, held, table, total, sems, table_sems = rest[blocks:]
    place_in, place_out = lax.axis_index(axes[0]), lax.axis_index(axes[1])
    copies = fill(table, [in_ref[place_in, n] for n in range(blocks)], given, table_sems)
    places_ref, others_ref = (rows_ref, cols_ref) if to_users else (cols_ref, rows_ref)

    def values(slot):
        return held[slot]

    def other(slot):
        return table[others_ref[slot]]

    left, right = (values, other) if to_users else (other, values)
    add_tiles(
        count_ref[0], vals_ref, held, sems, left, right, lambda slot: places_ref[slot], trash, total, copies
    )
    hand_out(total, [out_ref[place_out, n] for n in range(len(outs))], outs)


SMEM_WHOLE = pl.BlockSpec(memory_space=pltpu.SMEM)
TERM_VMEM = 52 * 2**20
HBM_WHOLE = pl.BlockSpec(memory_space=pltpu.HBM)


def tile_cost(vals, embed):
    slots, side = vals.shape[0], vals.shape[1]
    return pl.CostEstimate(
        flops=2 * slots * side * side * embed, bytes_accessed=2 * slots * side * side, transcendentals=0
    )


def terms(count, rows, cols, in_table, out_table, vals, blocks, axes, tiles, to_users):
    slots, side = vals.shape[0], vals.shape[1]
    group = group_of(slots)
    table = sum(block.shape[0] for block in blocks)
    tile = blocks[0].shape[1:]
    outs = out_table.shape[1]
    return pl.pallas_call(
        functools.partial(
            term_kernel, axes=axes, blocks=len(blocks), trash=tiles, to_users=to_users
        ),
        in_specs=[SMEM_WHOLE] * 5 + [HBM_WHOLE] + [pl.BlockSpec(memory_space=pl.ANY)] * len(blocks),
        out_specs=[VMEM_WHOLE] * outs,
        scratch_shapes=[
            pltpu.VMEM(vals.shape, BF16),
            pltpu.VMEM((table, *tile), BF16),
            pltpu.VMEM((tiles + 1, *tile), F32),
            pltpu.SemaphoreType.DMA((slots // group,)),
            pltpu.SemaphoreType.DMA((len(blocks),)),
        ],
        out_shape=[jax.ShapeDtypeStruct((tiles // outs, *tile), BF16) for _ in range(outs)],
        compiler_params=pltpu.CompilerParams(vmem_limit_bytes=TERM_VMEM),
        cost_estimate=tile_cost(vals, tile[1]),
        name="user_terms" if to_users else "item_terms",
    )(count, rows, cols, in_table, out_table, vals, *blocks)


def picked_rows(wanted_ref, low, out_ref, chunk):
    rows = low.shape[0]
    for at in range(0, wanted_ref.shape[0], chunk):
        some = min(chunk, wanted_ref.shape[0] - at)
        hot = wanted_ref[pl.ds(at, some), :] == lax.broadcasted_iota(jnp.int32, (some, rows), 1)
        out_ref[pl.ds(at, some), :] = jnp.dot(hot.astype(BF16), low, preferred_element_type=F32).astype(BF16)


def combine_kernel(emb_ref, wanted_ref, *rest, terms, transposed):
    parts = rest[:terms]
    final_ref, rows_ref = rest[terms:]
    side = parts[0].shape[-2]
    for i in range(parts[0].shape[0]):
        at = pl.ds(i * side, side)
        prop = functools.reduce(jnp.add, [part[i].astype(F32) for part in parts])
        if transposed:
            prop = prop.T
        final_ref[at, :] = (emb_ref[at, :] + prop) * 0.5
    picked_rows(wanted_ref, final_ref[...].astype(BF16), rows_ref, 256)


def combine(emb, parts, wanted, transposed, name):
    return pl.pallas_call(
        functools.partial(combine_kernel, terms=len(parts), transposed=transposed),
        in_specs=[VMEM_WHOLE] * (2 + len(parts)),
        out_specs=[VMEM_WHOLE] * 2,
        out_shape=[
            jax.ShapeDtypeStruct(emb.shape, F32),
            jax.ShapeDtypeStruct((wanted.shape[0], emb.shape[1]), BF16),
        ],
        compiler_params=pltpu.CompilerParams(vmem_limit_bytes=32 * 2**20),
        name=name,
    )(emb, wanted, *parts)


def bpr_kernel(user_slot_ref, item_slot_ref, users_ref, items_ref, negatives_ref, out_ref):
    def vectors(slot_ref, rows_ref):
        hot = slot_ref[...] == lax.broadcasted_iota(jnp.int32, (slot_ref.shape[0], rows_ref.shape[0]), 1)
        return jnp.dot(hot.astype(BF16), rows_ref[...], preferred_element_type=F32)

    users = vectors(user_slot_ref, users_ref)
    items = vectors(item_slot_ref, items_ref)
    positive = jnp.sum(users * items, axis=1, keepdims=True)
    against = lax.dot_general(
        users.astype(BF16), negatives_ref[...], (((1,), (1,)), ((), ())), preferred_element_type=F32
    )
    out_ref[...] = jnp.log1p(jnp.exp(against - positive))


def bpr(user_slot, item_slot, users, items, negatives):
    pairs, embed = user_slot.shape[0], users.shape[1]
    block = next(b for b in (128, 64, 32, 16, 8, pairs) if pairs % b == 0)
    whole = lambda array: pl.BlockSpec(array.shape, lambda i: (0, 0))
    return pl.pallas_call(
        bpr_kernel,
        grid=(pairs // block,),
        in_specs=[pl.BlockSpec((block, 1), lambda i: (i, 0))] * 2 + [whole(users), whole(items), whole(negatives)],
        out_specs=pl.BlockSpec((block, negatives.shape[0]), lambda i: (i, 0)),
        out_shape=jax.ShapeDtypeStruct((pairs, negatives.shape[0]), F32),
        compiler_params=pltpu.CompilerParams(
            dimension_semantics=("arbitrary",), vmem_limit_bytes=32 * 2**20
        ),
        name="bpr_terms",
    )(user_slot, item_slot, users, items, negatives)


def place_requests(owner, local, slots):
    pairs = owner.shape[0]
    order = jnp.arange(pairs, dtype=jnp.int32)
    same = (owner[:, None] == owner[None, :]) & (order[None, :] < order[:, None])
    slot = owner * slots + jnp.sum(same.astype(jnp.int32), axis=1)
    return slot


def requests_of(slot, local, total):
    hits = slot[:, None] == jnp.arange(total, dtype=jnp.int32)[None, :]
    return jnp.sum(jnp.where(hits, local[:, None], 0), axis=0)


def on_device(user_emb, item_emb, tile_vals, tile_rows, tile_cols, tile_count, pair_users, pair_items, negatives):
    row_count, col_count = lax.axis_size("row"), lax.axis_size("col")
    row, col = lax.axis_index("row"), lax.axis_index("col")
    devices = row_count * col_count
    user_dev, embed = user_emb.shape[2:]
    item_dev = item_emb.shape[2]
    side = tile_vals.shape[-1]
    user_tiles, item_tiles = user_dev // side, item_dev // side
    ring = ring_of(col_count)

    def ring_table(shifts):
        places = [[ring[(ring.index(c) + shift) % col_count] for shift in shifts] for c in range(col_count)]
        return np.asarray(places, np.int32) * user_tiles

    def around(array, shift):
        pairs = [(ring[p], ring[(p + shift) % col_count]) for p in range(col_count)]
        return lax.ppermute(array, "col", pairs)

    row_slow, row_fast = (row_count, 1) if row_count % 2 else (row_count // 2, 2)

    def row_table(steps):
        places = [
            [(r // row_fast + j) % row_slow * row_fast + (r + i) % row_fast for j, i in steps] for r in range(row_count)
        ]
        return np.asarray(places, np.int32) * item_tiles

    user_mine, item_mine = user_emb[0, 0], item_emb[0, 0]
    count, rows, cols = tile_count[0], tile_rows[0, 0], tile_cols[0, 0]
    vals = tile_vals[0, 0]
    user_low = jnp.swapaxes(user_mine.astype(BF16).reshape(user_tiles, side, embed), 1, 2)
    item_low = item_mine.astype(BF16).reshape(item_tiles, side, embed)

    def send_row(array, step):
        pairs = [
            (a * row_fast + b, step(a, b)[0] * row_fast + step(a, b)[1])
            for a in range(row_slow)
            for b in range(row_fast)
        ]
        return lax.ppermute(array, "row", pairs)

    halves = [item_low]
    for j in range(1, row_slow):
        halves.append(send_row(item_low, lambda a, b, j=j: ((a + j) % row_slow, b)))
    item_blocks = list(halves)
    item_steps = [(-j, 0) for j in range(row_slow)]
    for i in range(1, row_fast):
        for j, half in enumerate(halves):
            item_blocks.append(send_row(half, lambda a, b, i=i: (a, (b + i) % row_fast)))
            item_steps.append((-j, -i))

    slots = 2 * pair_users.shape[0] // devices
    user_owner, user_local = pair_users // user_dev, pair_users % user_dev
    item_holder, item_local = pair_items // item_dev, pair_items % item_dev
    item_owner = item_holder % row_count * col_count + item_holder // row_count
    user_slot = place_requests(user_owner, user_local, slots)
    item_slot = place_requests(item_owner, item_local, slots)
    asked = jnp.stack(
        [
            requests_of(user_slot, user_local, devices * slots).reshape(devices, slots),
            requests_of(item_slot, item_local, devices * slots).reshape(devices, slots),
        ],
        axis=1,
    )
    neg_each = negatives.shape[0] // devices
    offset = (col * row_count + row) * item_dev
    named = lax.dynamic_slice_in_dim(negatives, (row * col_count + col) * neg_each, neg_each, 0) - offset

    right, left = (col_count - 1) // 2, col_count // 2
    shifts = [0]
    for s in range(1, left + 1):
        shifts += [s] + ([-s] if s <= right else [])
    user_blocks = [(user_low, 0)]
    from_left = from_right = user_low
    part = None
    for s in range(1, left + 1):
        if s <= right:
            from_left = around(from_left, 1)
            user_blocks.append((from_left, -s))
        from_right = around(from_right, -1)
        user_blocks.append((from_right, s))
        if s == 1:
            tied = lax.optimization_barrier((item_blocks, from_left, from_right))
            user_parts = terms(
                count,
                rows,
                cols,
                row_table(item_steps),
                ring_table(shifts),
                vals,
                tied[0],
                ("row", "col"),
                col_count * user_tiles,
                True,
            )
            part = dict(zip(shifts, user_parts))
        if s == 2:
            from_left, from_right, part[0] = lax.optimization_barrier((from_left, from_right, part[0]))

    asked, part[0] = lax.optimization_barrier((asked, part[0]))
    wanted = lax.all_to_all(asked, ("row", "col"), split_axis=0, concat_axis=0, tiled=True)

    def plus(mine, more):
        return mine if more is None else (mine.astype(F32) + more.astype(F32)).astype(BF16)

    to_right = to_left = None
    for s in range(left, 0, -1):
        to_right = around(plus(part[s], to_right), 1)
        if s <= right:
            to_left = around(plus(part[-s], to_left), -1)
    user_terms_in = [part[0]] + [more for more in (to_right, to_left) if more is not None]

    out_steps = [(j, i) for j in range(row_slow) for i in range(row_fast)]
    item_out = terms(
        count,
        rows,
        cols,
        ring_table([shift for _, shift in user_blocks]),
        row_table(out_steps),
        vals,
        [block for block, _ in user_blocks],
        ("col", "row"),
        row_count * item_tiles,
        False,
    )
    item_sums = []
    for j in range(row_slow):
        mine = [item_out[j * row_fast]] + [
            send_row(item_out[j * row_fast + i], lambda a, b, i=i: (a, (b + i) % row_fast))
            for i in range(1, row_fast)
        ]
        if j:
            total = functools.reduce(jnp.add, [part.astype(F32) for part in mine]).astype(BF16)
            item_sums.append(send_row(total, lambda a, b, j=j: ((a + j) % row_slow, b)))
        else:
            item_sums += mine

    user_wanted = wanted[:, 0].reshape(-1, 1)
    item_wanted = jnp.concatenate([wanted[:, 1].reshape(-1), named]).reshape(-1, 1)

    item_final, item_rows = combine(item_mine, item_sums, item_wanted, True, "item_final")
    asked_rows = item_rows[: devices * slots].reshape(devices, slots, embed)
    named_rows = jnp.broadcast_to(item_rows[None, devices * slots :], (devices, neg_each, embed))
    item_back = lax.all_to_all(
        jnp.concatenate([asked_rows, named_rows], axis=1), ("row", "col"), split_axis=0, concat_axis=0, tiled=True
    )
    item_table_back = item_back[:, :slots].reshape(devices * slots, embed)
    negative_rows = item_back[:, slots:].reshape(devices * neg_each, embed)

    user_final, user_rows = combine(user_mine, user_terms_in, user_wanted, False, "user_final")
    user_back = lax.all_to_all(
        user_rows.reshape(devices, slots, embed), ("row", "col"), split_axis=0, concat_axis=0, tiled=True
    ).reshape(devices * slots, embed)
    bpr_terms = bpr(user_slot[:, None], item_slot[:, None], user_back, item_table_back, negative_rows)
    return user_final.reshape(user_emb.shape), item_final.reshape(item_emb.shape), bpr_terms


def solution(mesh):
    placed = (
        P("row", "col", None, None),
        P("col", "row", None, None),
        P("row", "col", None, None, None),
        P("row", "col", None),
        P("row", "col", None),
        P("row", "col"),
        P(("row", "col")),
        P(("row", "col")),
        P(),
    )
    return jax.shard_map(
        on_device,
        mesh=mesh,
        in_specs=placed,
        out_specs=(
            P("row", "col", None, None),
            P("col", "row", None, None),
            P(("row", "col"), None),
        ),
        check_vma=False,
    )
```

```python
import functools

import jax
import jax.numpy as jnp
import numpy as np
from jax import lax
from jax.experimental import pallas as pl
from jax.experimental.pallas import tpu as pltpu
from jax.sharding import PartitionSpec as P

F32 = jnp.float32
BF16 = jnp.bfloat16
VMEM_WHOLE = pl.BlockSpec(memory_space=pltpu.VMEM)


def split_axis(size):
    fast = max(d for d in range(1, size + 1) if size % d == 0 and d * d <= size)
    return size // fast, fast


def ring_of(size):
    slow, fast = split_axis(size)
    walk = [(a, 0) for a in range(slow)]
    for turn, a in enumerate(reversed(range(slow))):
        across = range(1, fast)
        walk += [(a, b) for b in (across if turn % 2 == 0 else reversed(across))]
    return [a * fast + b for a, b in walk]


def group_of(slots):
    return next(g for g in (64, 32, 16, 8, 4, 2, 1) if slots % g == 0)


def add_tiles(count, vals_hbm, held, sems, left, right, place, trash, total, before):
    most = sems.shape[0]
    group = held.shape[0] // most
    groups = (count + group - 1) // group

    def fetch(number):
        some = pl.ds(number * group, group)
        return pltpu.make_async_copy(vals_hbm.at[some], held.at[some], sems.at[number])

    def fetch_all(numbers):
        for number in numbers:

            @pl.when(number < groups)
            def _(number=number):
                fetch(number).start()

    fetch_all(range(1))
    total[...] = jnp.zeros_like(total)
    for copy in before:
        copy.wait()
    fetch_all(range(1, most))

    def one_group(number, carry):
        fetch(number).wait()
        products, places = [], []
        for u in range(group):
            slot = number * group + u
            products.append(jnp.dot(left(slot), right(slot), preferred_element_type=F32))
            places.append(jnp.where(slot < count, place(slot), trash))
        for product, at in zip(products, places):
            total[at] += product
        return carry

    lax.fori_loop(0, groups, one_group, 0)


def hand_out(total, bases, outs):
    for n, out in enumerate(outs):

        def tile(i, carry, n=n, out=out):
            out[i] = total[bases[n] + i].astype(BF16)
            return carry

        lax.fori_loop(0, out.shape[0], tile, 0, unroll=min(8, out.shape[0]))


def fill(table, bases, blocks, sems):
    copies = [
        pltpu.make_async_copy(block, table.at[pl.ds(base, block.shape[0])], sems.at[n])
        for n, (base, block) in enumerate(zip(bases, blocks))
    ]
    for copy in copies:
        copy.start()
    return copies


def term_kernel(count_ref, rows_ref, cols_ref, in_ref, out_ref, vals_ref, *rest, axes, blocks, trash, to_users):
    given = rest[:blocks]
    *outs, held, table, total, sems, table_sems = rest[blocks:]
    place_in, place_out = lax.axis_index(axes[0]), lax.axis_index(axes[1])
    copies = fill(table, [in_ref[place_in, n] for n in range(blocks)], given, table_sems)
    places_ref, others_ref = (rows_ref, cols_ref) if to_users else (cols_ref, rows_ref)

    def values(slot):
        return held[slot]

    def other(slot):
        return table[others_ref[slot]]

    left, right = (values, other) if to_users else (other, values)
    add_tiles(
        count_ref[0], vals_ref, held, sems, left, right, lambda slot: places_ref[slot], trash, total, copies
    )
    hand_out(total, [out_ref[place_out, n] for n in range(len(outs))], outs)


SMEM_WHOLE = pl.BlockSpec(memory_space=pltpu.SMEM)
TERM_VMEM = 52 * 2**20
HBM_WHOLE = pl.BlockSpec(memory_space=pltpu.HBM)


def tile_cost(vals, embed):
    slots, side = vals.shape[0], vals.shape[1]
    return pl.CostEstimate(
        flops=2 * slots * side * side * embed, bytes_accessed=2 * slots * side * side, transcendentals=0
    )


def terms(count, rows, cols, in_table, out_table, vals, blocks, axes, tiles, to_users):
    slots, side = vals.shape[0], vals.shape[1]
    group = group_of(slots)
    table = sum(block.shape[0] for block in blocks)
    tile = blocks[0].shape[1:]
    outs = out_table.shape[1]
    return pl.pallas_call(
        functools.partial(
            term_kernel, axes=axes, blocks=len(blocks), trash=tiles, to_users=to_users
        ),
        in_specs=[SMEM_WHOLE] * 5 + [HBM_WHOLE] + [pl.BlockSpec(memory_space=pl.ANY)] * len(blocks),
        out_specs=[VMEM_WHOLE] * outs,
        scratch_shapes=[
            pltpu.VMEM(vals.shape, BF16),
            pltpu.VMEM((table, *tile), BF16),
            pltpu.VMEM((tiles + 1, *tile), F32),
            pltpu.SemaphoreType.DMA((slots // group,)),
            pltpu.SemaphoreType.DMA((len(blocks),)),
        ],
        out_shape=[jax.ShapeDtypeStruct((tiles // outs, *tile), BF16) for _ in range(outs)],
        compiler_params=pltpu.CompilerParams(vmem_limit_bytes=TERM_VMEM),
        cost_estimate=tile_cost(vals, tile[1]),
        name="user_terms" if to_users else "item_terms",
    )(count, rows, cols, in_table, out_table, vals, *blocks)


def picked_rows(wanted_ref, low, out_ref, chunk):
    rows = low.shape[0]
    for at in range(0, wanted_ref.shape[0], chunk):
        some = min(chunk, wanted_ref.shape[0] - at)
        hot = wanted_ref[pl.ds(at, some), :] == lax.broadcasted_iota(jnp.int32, (some, rows), 1)
        out_ref[pl.ds(at, some), :] = jnp.dot(hot.astype(BF16), low, preferred_element_type=F32).astype(BF16)


def combine_kernel(emb_ref, wanted_ref, *rest, terms, transposed):
    parts = rest[:terms]
    final_ref, rows_ref = rest[terms:]
    side = parts[0].shape[-2]
    for i in range(parts[0].shape[0]):
        at = pl.ds(i * side, side)
        prop = functools.reduce(jnp.add, [part[i].astype(F32) for part in parts])
        if transposed:
            prop = prop.T
        final_ref[at, :] = (emb_ref[at, :] + prop) * 0.5
    picked_rows(wanted_ref, final_ref[...].astype(BF16), rows_ref, 512)


def combine(emb, parts, wanted, transposed, name):
    return pl.pallas_call(
        functools.partial(combine_kernel, terms=len(parts), transposed=transposed),
        in_specs=[VMEM_WHOLE] * (2 + len(parts)),
        out_specs=[VMEM_WHOLE] * 2,
        out_shape=[
            jax.ShapeDtypeStruct(emb.shape, F32),
            jax.ShapeDtypeStruct((wanted.shape[0], emb.shape[1]), BF16),
        ],
        compiler_params=pltpu.CompilerParams(vmem_limit_bytes=32 * 2**20),
        name=name,
    )(emb, wanted, *parts)


def bpr_kernel(user_slot_ref, item_slot_ref, users_ref, items_ref, negatives_ref, out_ref):
    def vectors(slot_ref, rows_ref):
        hot = slot_ref[...] == lax.broadcasted_iota(jnp.int32, (slot_ref.shape[0], rows_ref.shape[0]), 1)
        return jnp.dot(hot.astype(BF16), rows_ref[...], preferred_element_type=F32)

    users = vectors(user_slot_ref, users_ref)
    items = vectors(item_slot_ref, items_ref)
    positive = jnp.sum(users * items, axis=1, keepdims=True)
    against = lax.dot_general(
        users.astype(BF16), negatives_ref[...], (((1,), (1,)), ((), ())), preferred_element_type=F32
    )
    out_ref[...] = jnp.log1p(jnp.exp(against - positive))


def bpr(user_slot, item_slot, users, items, negatives):
    pairs, embed = user_slot.shape[0], users.shape[1]
    block = next(b for b in (256, 128, 64, 32, 16, 8, pairs) if pairs % b == 0)
    whole = lambda array: pl.BlockSpec(array.shape, lambda i: (0, 0))
    return pl.pallas_call(
        bpr_kernel,
        grid=(pairs // block,),
        in_specs=[pl.BlockSpec((block, 1), lambda i: (i, 0))] * 2 + [whole(users), whole(items), whole(negatives)],
        out_specs=pl.BlockSpec((block, negatives.shape[0]), lambda i: (i, 0)),
        out_shape=jax.ShapeDtypeStruct((pairs, negatives.shape[0]), F32),
        compiler_params=pltpu.CompilerParams(
            dimension_semantics=("arbitrary",), vmem_limit_bytes=32 * 2**20
        ),
        name="bpr_terms",
    )(user_slot, item_slot, users, items, negatives)


def place_requests(owner, local, slots):
    pairs = owner.shape[0]
    order = jnp.arange(pairs, dtype=jnp.int32)
    same = (owner[:, None] == owner[None, :]) & (order[None, :] < order[:, None])
    slot = owner * slots + jnp.sum(same.astype(jnp.int32), axis=1)
    return slot


def requests_of(slot, local, total):
    hits = slot[:, None] == jnp.arange(total, dtype=jnp.int32)[None, :]
    return jnp.sum(jnp.where(hits, local[:, None], 0), axis=0)


def after(arrays, *ahead):
    return lax.optimization_barrier((arrays, ahead))[0]


def on_device(user_emb, item_emb, tile_vals, tile_rows, tile_cols, tile_count, pair_users, pair_items, negatives):
    row_count, col_count = lax.axis_size("row"), lax.axis_size("col")
    row, col = lax.axis_index("row"), lax.axis_index("col")
    devices = row_count * col_count
    user_dev, embed = user_emb.shape[2:]
    item_dev = item_emb.shape[2]
    side = tile_vals.shape[-1]
    user_tiles, item_tiles = user_dev // side, item_dev // side
    ring = ring_of(col_count)

    def ring_table(shifts):
        places = [[ring[(ring.index(c) + shift) % col_count] for shift in shifts] for c in range(col_count)]
        return np.asarray(places, np.int32) * user_tiles

    def around(array, shift):
        pairs = [(ring[p], ring[(p + shift) % col_count]) for p in range(col_count)]
        return lax.ppermute(array, "col", pairs)

    row_slow, row_fast = (row_count, 1) if row_count % 2 else (row_count // 2, 2)

    def row_table(steps):
        places = [
            [(r // row_fast + j) % row_slow * row_fast + (r + i) % row_fast for j, i in steps] for r in range(row_count)
        ]
        return np.asarray(places, np.int32) * item_tiles

    user_mine, item_mine = user_emb[0, 0], item_emb[0, 0]
    count, rows, cols = tile_count[0], tile_rows[0, 0], tile_cols[0, 0]
    vals = tile_vals[0, 0]
    user_low = jnp.swapaxes(user_mine.astype(BF16).reshape(user_tiles, side, embed), 1, 2)
    item_low = item_mine.astype(BF16).reshape(item_tiles, side, embed)

    def send_row(array, step):
        pairs = [
            (a * row_fast + b, step(a, b)[0] * row_fast + step(a, b)[1])
            for a in range(row_slow)
            for b in range(row_fast)
        ]
        return lax.ppermute(array, "row", pairs)

    halves = [item_low]
    for j in range(1, row_slow):
        halves.append(send_row(item_low, lambda a, b, j=j: ((a + j) % row_slow, b)))
    item_blocks = list(halves)
    item_steps = [(-j, 0) for j in range(row_slow)]
    for i in range(1, row_fast):
        for j, half in enumerate(halves):
            item_blocks.append(send_row(half, lambda a, b, i=i: (a, (b + i) % row_fast)))
            item_steps.append((-j, -i))

    slots = 2 * pair_users.shape[0] // devices
    user_owner, user_local = pair_users // user_dev, pair_users % user_dev
    item_holder, item_local = pair_items // item_dev, pair_items % item_dev
    item_owner = item_holder % row_count * col_count + item_holder // row_count
    user_slot = place_requests(user_owner, user_local, slots)
    item_slot = place_requests(item_owner, item_local, slots)
    asked = jnp.stack(
        [
            requests_of(user_slot, user_local, devices * slots).reshape(devices, slots),
            requests_of(item_slot, item_local, devices * slots).reshape(devices, slots),
        ],
        axis=1,
    )
    neg_each = negatives.shape[0] // devices
    offset = (col * row_count + row) * item_dev
    named = lax.dynamic_slice_in_dim(negatives, (row * col_count + col) * neg_each, neg_each, 0) - offset

    right, left = (col_count - 1) // 2, col_count // 2
    shifts = [0]
    for s in range(1, left + 1):
        shifts += [s] + ([-s] if s <= right else [])
    user_blocks = [(user_low, 0)]
    from_left = from_right = user_low
    part = None
    for s in range(1, left + 1):
        if s <= right:
            from_left = around(from_left, 1)
            user_blocks.append((from_left, -s))
        from_right = around(from_right, -1)
        user_blocks.append((from_right, s))
        if s == 1:
            tied = lax.optimization_barrier((item_blocks, from_left, from_right))
            user_parts = terms(
                count,
                rows,
                cols,
                row_table(item_steps),
                ring_table(shifts),
                vals,
                tied[0],
                ("row", "col"),
                col_count * user_tiles,
                True,
            )
            part = dict(zip(shifts, user_parts))
        if s == 2:
            from_left, from_right, part[0] = lax.optimization_barrier((from_left, from_right, part[0]))

    asked, part[0] = lax.optimization_barrier((asked, part[0]))
    wanted = lax.all_to_all(asked, ("row", "col"), split_axis=0, concat_axis=0, tiled=True)

    def plus(mine, more):
        return mine if more is None else (mine.astype(F32) + more.astype(F32)).astype(BF16)

    to_right = to_left = None
    for s in range(left, 0, -1):
        to_right = around(plus(part[s], to_right), 1)
        if s <= right:
            mine = part[-s] if to_left is not None else after(part[-s], from_right)
            to_left = around(plus(mine, to_left), -1)
    user_terms_in = [part[0]] + [more for more in (to_right, to_left) if more is not None]

    out_steps = [(j, i) for j in range(row_slow) for i in range(row_fast)]
    item_out = terms(
        count,
        rows,
        cols,
        ring_table([shift for _, shift in user_blocks]),
        row_table(out_steps),
        vals,
        [block for block, _ in user_blocks],
        ("col", "row"),
        row_count * item_tiles,
        False,
    )
    item_sums = []
    for j in range(row_slow):
        mine = [item_out[j * row_fast]] + [
            send_row(item_out[j * row_fast + i], lambda a, b, i=i: (a, (b + i) % row_fast))
            for i in range(1, row_fast)
        ]
        if j:
            total = functools.reduce(jnp.add, [part.astype(F32) for part in mine]).astype(BF16)
            item_sums.append(send_row(total, lambda a, b, j=j: ((a + j) % row_slow, b)))
        else:
            item_sums += mine

    user_wanted = wanted[:, 0].reshape(-1, 1)
    item_wanted = jnp.concatenate([wanted[:, 1].reshape(-1), named]).reshape(-1, 1)

    item_final, item_rows = combine(item_mine, item_sums, item_wanted, True, "item_final")
    asked_rows = item_rows[: devices * slots].reshape(devices, slots, embed)
    named_rows = jnp.broadcast_to(item_rows[None, devices * slots :], (devices, neg_each, embed))
    item_back = lax.all_to_all(
        jnp.concatenate([asked_rows, named_rows], axis=1), ("row", "col"), split_axis=0, concat_axis=0, tiled=True
    )
    item_table_back = item_back[:, :slots].reshape(devices * slots, embed)
    negative_rows = item_back[:, slots:].reshape(devices * neg_each, embed)

    user_final, user_rows = combine(user_mine, user_terms_in, user_wanted, False, "user_final")
    user_back = lax.all_to_all(
        user_rows.reshape(devices, slots, embed), ("row", "col"), split_axis=0, concat_axis=0, tiled=True
    ).reshape(devices * slots, embed)
    bpr_terms = bpr(user_slot[:, None], item_slot[:, None], user_back, item_table_back, negative_rows)
    return user_final.reshape(user_emb.shape), item_final.reshape(item_emb.shape), bpr_terms


def solution(mesh):
    placed = (
        P("row", "col", None, None),
        P("col", "row", None, None),
        P("row", "col", None, None, None),
        P("row", "col", None),
        P("row", "col", None),
        P("row", "col"),
        P(("row", "col")),
        P(("row", "col")),
        P(),
    )
    return jax.shard_map(
        on_device,
        mesh=mesh,
        in_specs=placed,
        out_specs=(
            P("row", "col", None, None),
            P("col", "row", None, None),
            P(("row", "col"), None),
        ),
        check_vma=False,
    )
```

```python
import functools

import jax
import jax.numpy as jnp
import numpy as np
from jax import lax
from jax.experimental import pallas as pl
from jax.experimental.pallas import tpu as pltpu
from jax.sharding import PartitionSpec as P

F32 = jnp.float32
BF16 = jnp.bfloat16
VMEM_WHOLE = pl.BlockSpec(memory_space=pltpu.VMEM)


def split_axis(size):
    fast = max(d for d in range(1, size + 1) if size % d == 0 and d * d <= size)
    return size // fast, fast


def ring_of(size):
    slow, fast = split_axis(size)
    walk = [(a, 0) for a in range(slow)]
    for turn, a in enumerate(reversed(range(slow))):
        across = range(1, fast)
        walk += [(a, b) for b in (across if turn % 2 == 0 else reversed(across))]
    return [a * fast + b for a, b in walk]


def group_of(slots):
    return next(g for g in (64, 32, 16, 8, 4, 2, 1) if slots % g == 0)


def add_tiles(count, vals_hbm, held, sems, left, right, place, trash, total, before):
    most = sems.shape[0]
    group = held.shape[0] // most
    groups = (count + group - 1) // group

    def fetch(number):
        some = pl.ds(number * group, group)
        return pltpu.make_async_copy(vals_hbm.at[some], held.at[some], sems.at[number])

    def fetch_all(numbers):
        for number in numbers:

            @pl.when(number < groups)
            def _(number=number):
                fetch(number).start()

    fetch_all(range(1))
    total[...] = jnp.zeros_like(total)
    for copy in before:
        copy.wait()
    fetch_all(range(1, most))

    def one_group(number, carry):
        fetch(number).wait()
        products, places = [], []
        for u in range(group):
            slot = number * group + u
            products.append(jnp.dot(left(slot), right(slot), preferred_element_type=F32))
            places.append(jnp.where(slot < count, place(slot), trash))
        for product, at in zip(products, places):
            total[at] += product
        return carry

    lax.fori_loop(0, groups, one_group, 0)


def hand_out(total, bases, outs):
    for n, out in enumerate(outs):

        def tile(i, carry, n=n, out=out):
            out[i] = total[bases[n] + i].astype(BF16)
            return carry

        lax.fori_loop(0, out.shape[0], tile, 0, unroll=min(8, out.shape[0]))


def fill(table, bases, blocks, sems):
    copies = [
        pltpu.make_async_copy(block, table.at[pl.ds(base, block.shape[0])], sems.at[n])
        for n, (base, block) in enumerate(zip(bases, blocks))
    ]
    for copy in copies:
        copy.start()
    return copies


def term_kernel(count_ref, rows_ref, cols_ref, in_ref, out_ref, vals_ref, *rest, axes, blocks, trash, to_users):
    given = rest[:blocks]
    *outs, held, table, total, sems, table_sems = rest[blocks:]
    place_in, place_out = lax.axis_index(axes[0]), lax.axis_index(axes[1])
    copies = fill(table, [in_ref[place_in, n] for n in range(blocks)], given, table_sems)
    places_ref, others_ref = (rows_ref, cols_ref) if to_users else (cols_ref, rows_ref)

    def values(slot):
        return held[slot]

    def other(slot):
        return table[others_ref[slot]]

    left, right = (values, other) if to_users else (other, values)
    add_tiles(
        count_ref[0], vals_ref, held, sems, left, right, lambda slot: places_ref[slot], trash, total, copies
    )
    hand_out(total, [out_ref[place_out, n] for n in range(len(outs))], outs)


SMEM_WHOLE = pl.BlockSpec(memory_space=pltpu.SMEM)
TERM_VMEM = 52 * 2**20
HBM_WHOLE = pl.BlockSpec(memory_space=pltpu.HBM)


def tile_cost(vals, embed):
    slots, side = vals.shape[0], vals.shape[1]
    return pl.CostEstimate(
        flops=2 * slots * side * side * embed, bytes_accessed=2 * slots * side * side, transcendentals=0
    )


def terms(count, rows, cols, in_table, out_table, vals, blocks, axes, tiles, to_users):
    slots, side = vals.shape[0], vals.shape[1]
    group = group_of(slots)
    table = sum(block.shape[0] for block in blocks)
    tile = blocks[0].shape[1:]
    outs = out_table.shape[1]
    return pl.pallas_call(
        functools.partial(
            term_kernel, axes=axes, blocks=len(blocks), trash=tiles, to_users=to_users
        ),
        in_specs=[SMEM_WHOLE] * 5 + [HBM_WHOLE] + [pl.BlockSpec(memory_space=pl.ANY)] * len(blocks),
        out_specs=[VMEM_WHOLE] * outs,
        scratch_shapes=[
            pltpu.VMEM(vals.shape, BF16),
            pltpu.VMEM((table, *tile), BF16),
            pltpu.VMEM((tiles + 1, *tile), F32),
            pltpu.SemaphoreType.DMA((slots // group,)),
            pltpu.SemaphoreType.DMA((len(blocks),)),
        ],
        out_shape=[jax.ShapeDtypeStruct((tiles // outs, *tile), BF16) for _ in range(outs)],
        compiler_params=pltpu.CompilerParams(vmem_limit_bytes=TERM_VMEM),
        cost_estimate=tile_cost(vals, tile[1]),
        name="user_terms" if to_users else "item_terms",
    )(count, rows, cols, in_table, out_table, vals, *blocks)


def picked_rows(wanted_ref, low, out_ref, chunk):
    rows = low.shape[0]
    for at in range(0, wanted_ref.shape[0], chunk):
        some = min(chunk, wanted_ref.shape[0] - at)
        hot = wanted_ref[pl.ds(at, some), :] == lax.broadcasted_iota(jnp.int32, (some, rows), 1)
        out_ref[pl.ds(at, some), :] = jnp.dot(hot.astype(BF16), low, preferred_element_type=F32).astype(BF16)


def combine_kernel(emb_ref, wanted_ref, *rest, terms, transposed):
    parts = rest[:terms]
    final_ref, rows_ref = rest[terms:]
    side = parts[0].shape[-2]
    for i in range(parts[0].shape[0]):
        at = pl.ds(i * side, side)
        prop = functools.reduce(jnp.add, [part[i].astype(F32) for part in parts])
        if transposed:
            prop = prop.T
        final_ref[at, :] = (emb_ref[at, :] + prop) * 0.5
    picked_rows(wanted_ref, final_ref[...].astype(BF16), rows_ref, 512)


def combine(emb, parts, wanted, transposed, name):
    return pl.pallas_call(
        functools.partial(combine_kernel, terms=len(parts), transposed=transposed),
        in_specs=[VMEM_WHOLE] * (2 + len(parts)),
        out_specs=[VMEM_WHOLE] * 2,
        out_shape=[
            jax.ShapeDtypeStruct(emb.shape, F32),
            jax.ShapeDtypeStruct((wanted.shape[0], emb.shape[1]), BF16),
        ],
        compiler_params=pltpu.CompilerParams(vmem_limit_bytes=32 * 2**20),
        name=name,
    )(emb, wanted, *parts)


def slot_rows(slot_ref, rows_ref):
    hot = slot_ref[...] == lax.broadcasted_iota(jnp.int32, (slot_ref.shape[0], rows_ref.shape[0]), 1)
    return jnp.dot(hot.astype(BF16), rows_ref[...], preferred_element_type=F32)


def item_vectors_kernel(slot_ref, rows_ref, out_ref):
    out_ref[...] = slot_rows(slot_ref, rows_ref).astype(BF16)


def item_vectors(slot, rows):
    return pl.pallas_call(
        item_vectors_kernel,
        in_specs=[VMEM_WHOLE] * 2,
        out_specs=VMEM_WHOLE,
        out_shape=jax.ShapeDtypeStruct((slot.shape[0], rows.shape[1]), BF16),
        compiler_params=pltpu.CompilerParams(vmem_limit_bytes=32 * 2**20),
        cost_estimate=pl.CostEstimate(flops=1, bytes_accessed=1, transcendentals=0),
        name="item_vectors",
    )(slot, rows)


def bpr_kernel(user_slot_ref, users_ref, items_ref, negatives_ref, out_ref):
    users = slot_rows(user_slot_ref, users_ref)
    positive = jnp.sum(users * items_ref[...].astype(F32), axis=1, keepdims=True)
    against = lax.dot_general(
        users.astype(BF16), negatives_ref[...], (((1,), (1,)), ((), ())), preferred_element_type=F32
    )
    out_ref[...] = jnp.log1p(jnp.exp(against - positive))


def bpr(user_slot, users, items, negatives):
    pairs, embed = user_slot.shape[0], users.shape[1]
    block = next(b for b in (256, 128, 64, 32, 16, 8, pairs) if pairs % b == 0)
    whole = lambda array: pl.BlockSpec(array.shape, lambda i: (0, 0))
    return pl.pallas_call(
        bpr_kernel,
        grid=(pairs // block,),
        in_specs=[
            pl.BlockSpec((block, 1), lambda i: (i, 0)),
            whole(users),
            pl.BlockSpec((block, embed), lambda i: (i, 0)),
            whole(negatives),
        ],
        out_specs=pl.BlockSpec((block, negatives.shape[0]), lambda i: (i, 0)),
        out_shape=jax.ShapeDtypeStruct((pairs, negatives.shape[0]), F32),
        compiler_params=pltpu.CompilerParams(
            dimension_semantics=("arbitrary",), vmem_limit_bytes=32 * 2**20
        ),
        name="bpr_terms",
    )(user_slot, users, items, negatives)


def place_requests(owner, local, slots):
    pairs = owner.shape[0]
    order = jnp.arange(pairs, dtype=jnp.int32)
    same = (owner[:, None] == owner[None, :]) & (order[None, :] < order[:, None])
    slot = owner * slots + jnp.sum(same.astype(jnp.int32), axis=1)
    return slot


def requests_of(slot, local, total):
    hits = slot[:, None] == jnp.arange(total, dtype=jnp.int32)[None, :]
    return jnp.sum(jnp.where(hits, local[:, None], 0), axis=0)


def after(arrays, *ahead):
    return lax.optimization_barrier((arrays, ahead))[0]


def on_device(user_emb, item_emb, tile_vals, tile_rows, tile_cols, tile_count, pair_users, pair_items, negatives):
    row_count, col_count = lax.axis_size("row"), lax.axis_size("col")
    row, col = lax.axis_index("row"), lax.axis_index("col")
    devices = row_count * col_count
    user_dev, embed = user_emb.shape[2:]
    item_dev = item_emb.shape[2]
    side = tile_vals.shape[-1]
    user_tiles, item_tiles = user_dev // side, item_dev // side
    ring = ring_of(col_count)

    def ring_table(shifts):
        places = [[ring[(ring.index(c) + shift) % col_count] for shift in shifts] for c in range(col_count)]
        return np.asarray(places, np.int32) * user_tiles

    def around(array, shift):
        pairs = [(ring[p], ring[(p + shift) % col_count]) for p in range(col_count)]
        return lax.ppermute(array, "col", pairs)

    row_slow, row_fast = (row_count, 1) if row_count % 2 else (row_count // 2, 2)

    def row_table(steps):
        places = [
            [(r // row_fast + j) % row_slow * row_fast + (r + i) % row_fast for j, i in steps] for r in range(row_count)
        ]
        return np.asarray(places, np.int32) * item_tiles

    user_mine, item_mine = user_emb[0, 0], item_emb[0, 0]
    count, rows, cols = tile_count[0], tile_rows[0, 0], tile_cols[0, 0]
    vals = tile_vals[0, 0]
    user_low = jnp.swapaxes(user_mine.astype(BF16).reshape(user_tiles, side, embed), 1, 2)
    item_low = item_mine.astype(BF16).reshape(item_tiles, side, embed)

    def send_row(array, step):
        pairs = [
            (a * row_fast + b, step(a, b)[0] * row_fast + step(a, b)[1])
            for a in range(row_slow)
            for b in range(row_fast)
        ]
        return lax.ppermute(array, "row", pairs)

    halves = [item_low]
    for j in range(1, row_slow):
        halves.append(send_row(item_low, lambda a, b, j=j: ((a + j) % row_slow, b)))
    item_blocks = list(halves)
    item_steps = [(-j, 0) for j in range(row_slow)]
    for i in range(1, row_fast):
        for j, half in enumerate(halves):
            item_blocks.append(send_row(half, lambda a, b, i=i: (a, (b + i) % row_fast)))
            item_steps.append((-j, -i))

    slots = 2 * pair_users.shape[0] // devices
    user_owner, user_local = pair_users // user_dev, pair_users % user_dev
    item_holder, item_local = pair_items // item_dev, pair_items % item_dev
    item_owner = item_holder % row_count * col_count + item_holder // row_count
    user_slot = place_requests(user_owner, user_local, slots)
    item_slot = place_requests(item_owner, item_local, slots)
    asked = jnp.stack(
        [
            requests_of(user_slot, user_local, devices * slots).reshape(devices, slots),
            requests_of(item_slot, item_local, devices * slots).reshape(devices, slots),
        ],
        axis=1,
    )
    neg_each = negatives.shape[0] // devices
    offset = (col * row_count + row) * item_dev
    named = lax.dynamic_slice_in_dim(negatives, (row * col_count + col) * neg_each, neg_each, 0) - offset

    right, left = (col_count - 1) // 2, col_count // 2
    shifts = [0]
    for s in range(1, left + 1):
        shifts += [s] + ([-s] if s <= right else [])
    user_blocks = [(user_low, 0)]
    from_left = from_right = user_low
    part = None
    for s in range(1, left + 1):
        if s <= right:
            from_left = around(from_left, 1)
            user_blocks.append((from_left, -s))
        from_right = around(from_right, -1)
        user_blocks.append((from_right, s))
        if s == 1:
            tied = lax.optimization_barrier((item_blocks, from_left, from_right))
            user_parts = terms(
                count,
                rows,
                cols,
                row_table(item_steps),
                ring_table(shifts),
                vals,
                tied[0],
                ("row", "col"),
                col_count * user_tiles,
                True,
            )
            part = dict(zip(shifts, user_parts))
        if s == 2:
            from_left, from_right, part[0] = lax.optimization_barrier((from_left, from_right, part[0]))

    asked, part[0] = lax.optimization_barrier((asked, part[0]))
    wanted = lax.all_to_all(asked, ("row", "col"), split_axis=0, concat_axis=0, tiled=True)

    def plus(mine, more):
        return mine if more is None else (mine.astype(F32) + more.astype(F32)).astype(BF16)

    to_right = to_left = None
    for s in range(left, 0, -1):
        to_right = around(plus(part[s], to_right), 1)
        if s <= right:
            mine = part[-s] if to_left is not None else after(part[-s], from_right)
            to_left = around(plus(mine, to_left), -1)
    user_terms_in = [part[0]] + [more for more in (to_right, to_left) if more is not None]

    out_steps = [(j, i) for j in range(row_slow) for i in range(row_fast)]
    item_out = terms(
        count,
        rows,
        cols,
        ring_table([shift for _, shift in user_blocks]),
        row_table(out_steps),
        vals,
        [block for block, _ in user_blocks],
        ("col", "row"),
        row_count * item_tiles,
        False,
    )
    item_sums = []
    for j in range(row_slow):
        mine = [item_out[j * row_fast]] + [
            send_row(item_out[j * row_fast + i], lambda a, b, i=i: (a, (b + i) % row_fast))
            for i in range(1, row_fast)
        ]
        if j:
            total = functools.reduce(jnp.add, [part.astype(F32) for part in mine]).astype(BF16)
            item_sums.append(send_row(total, lambda a, b, j=j: ((a + j) % row_slow, b)))
        else:
            item_sums += mine

    user_wanted = wanted[:, 0].reshape(-1, 1)
    item_wanted = jnp.concatenate([wanted[:, 1].reshape(-1), named]).reshape(-1, 1)

    item_final, item_rows = combine(item_mine, item_sums, item_wanted, True, "item_final")
    asked_rows = item_rows[: devices * slots].reshape(devices, slots, embed)
    named_rows = jnp.broadcast_to(item_rows[None, devices * slots :], (devices, neg_each, embed))
    item_back = lax.all_to_all(
        jnp.concatenate([asked_rows, named_rows], axis=1), ("row", "col"), split_axis=0, concat_axis=0, tiled=True
    )
    item_table_back = item_back[:, :slots].reshape(devices * slots, embed)
    negative_rows = item_back[:, slots:].reshape(devices * neg_each, embed)

    user_final, user_rows = combine(user_mine, user_terms_in, user_wanted, False, "user_final")
    user_back = lax.all_to_all(
        user_rows.reshape(devices, slots, embed), ("row", "col"), split_axis=0, concat_axis=0, tiled=True
    ).reshape(devices * slots, embed)
    items = item_vectors(item_slot[:, None], item_table_back)
    bpr_terms = bpr(user_slot[:, None], user_back, items, negative_rows)
    return user_final.reshape(user_emb.shape), item_final.reshape(item_emb.shape), bpr_terms


def solution(mesh):
    placed = (
        P("row", "col", None, None),
        P("col", "row", None, None),
        P("row", "col", None, None, None),
        P("row", "col", None),
        P("row", "col", None),
        P("row", "col"),
        P(("row", "col")),
        P(("row", "col")),
        P(),
    )
    return jax.shard_map(
        on_device,
        mesh=mesh,
        in_specs=placed,
        out_specs=(
            P("row", "col", None, None),
            P("col", "row", None, None),
            P(("row", "col"), None),
        ),
        check_vma=False,
    )
```
